512 devices in a mesh: ctx: 32 (over x_lo, z), tp: 16 (over x_hi, y, core).
Axes of the slice: x: 4 (x_hi: 2, x_lo: 2; x = x_hi * 2 + x_lo), y: 4, z: 16, core: 2. Of those that a mesh axis runs over, the one named last changes fastest.
Arguments:
- queries: bfloat16 [512, 128, 576], P('ctx', 'tp'), may hold values from -90 to 90
- grad_out: bfloat16 [512, 128, 512], P('ctx', 'tp'), may hold values from -6 to 6
- latent_cache: bfloat16 [4096, 576], P('ctx'), may hold values from -6 to 6
- slab_starts: int32 [32], P('ctx'), may hold values from 0 to 4080, as said below
Outputs:
- query_grad: bfloat16 [512, 128, 576], P('ctx', 'tp')
- cache_grad: float32 [4096, 576], P('ctx')
The draws below stay inside these ranges and needn't reach their ends.
Inputs may be any that keep to these rules, and one draw needn't show every extreme that they name: `slab_starts`: some slab starts at 0 and some at 4080.
All inputs are finite; a program needn't handle non-finite values.
Results may differ from the reference program's by a relative error of at most 0.0049.
Values may be sent and summed in bfloat16 or wider, within the bound.
A program may use at most 64 MiB of HBM per device.

```python
import jax
import jax.numpy as jnp
from jax import lax

HEADS = 128
LATENT = 512
ROPE = 64
NOPE = 128
Q_DEV = 16
SLABS = 32
SEQ = 4096
QUERIES = 512


def shared_cache(key):
    return jnp.clip(jax.random.normal(key, (SEQ, LATENT + ROPE), jnp.float32), -6.0, 6.0)


def shared_starts(key):
    own_key = jax.random.fold_in(key, 101)
    starts = jax.random.randint(jax.random.fold_in(own_key, 1), (SLABS,), 0, SEQ - Q_DEV + 1)
    order = jax.random.permutation(jax.random.fold_in(own_key, 2), SLABS)
    starts = starts.at[order[0]].set(SEQ - Q_DEV)
    return starts.at[order[1]].set(0)


def draw_slab_starts(key, part):
    starts = shared_starts(key)
    return starts.astype(jnp.int32)


def draw_latent_cache(key, part):
    return shared_cache(key).astype(jnp.bfloat16)


def draw_queries(key, part):
    key = jax.random.fold_in(key, 7)
    full_width = LATENT + ROPE
    base = jnp.clip(jax.random.normal(key, (QUERIES, HEADS, full_width), jnp.float32), -6.0, 6.0)
    return base.astype(jnp.bfloat16)


def shard_levels(rng, shape, pieces, smallest, high):
    def one(axis_at, blocks):
        draws = jax.random.uniform(jax.random.fold_in(jax.random.fold_in(rng, 6), axis_at), (blocks,), jnp.float32, smallest / len(pieces), high / len(pieces))
        return jnp.repeat(jnp.exp(draws), shape[axis_at] // blocks).reshape((-1,) + (1,) * (len(shape) - axis_at - 1))

    gain = one(*pieces[0])
    for cut in pieces[1:]:
        gain = gain * one(*cut)
    return gain


def normal_values(key, extent, deviation, bound, split=(), held_as=jnp.bfloat16):
    array = jax.random.normal(key, extent, jnp.float32) * deviation
    if len(split) > 0:
        array = shard_levels(key, extent, split, -0.22, 0.18) * array
    return jnp.clip(array, min=-bound, max=bound).astype(held_as)


def setup_inputs(seed: int = 0) -> dict:
    splits = jax.random.split(jax.random.key(seed), 5)
    return {
        "queries": draw_queries(jax.random.fold_in(splits[4], 71), 0),
        "grad_out": normal_values(splits[1], (QUERIES, HEADS, LATENT), 1.0, 6.0, ((0, 32), (1, 16))),
        "latent_cache": draw_latent_cache(jax.random.fold_in(splits[4], 71), 0),
        "slab_starts": draw_slab_starts(jax.random.fold_in(splits[4], 71), 0),
    }


def reference(queries, grad_out, latent_cache, slab_starts):
    score_scale = (NOPE + ROPE) ** -0.5
    positions = (slab_starts[:, None] + jnp.arange(Q_DEV, dtype=jnp.int32)[None, :]).reshape(-1)
    key_pos = jnp.arange(SEQ, dtype=jnp.int32)
    visible = key_pos[None, :] <= positions[:, None]
    value_cols = latent_cache[:, :LATENT]

    def one_head(grad_total, head_index):
        query_head = lax.dynamic_index_in_dim(queries, head_index, 1, keepdims=False)
        cotan_head = lax.dynamic_index_in_dim(grad_out, head_index, 1, keepdims=False)
        scores = jnp.dot(query_head, latent_cache.T, preferred_element_type=jnp.float32) * score_scale
        scores = jnp.where(visible, scores, -jnp.inf)
        row_max = jnp.max(scores, axis=1)
        log_total = row_max + jnp.log(jnp.sum(jnp.exp(scores - row_max[:, None]), axis=1))
        probs = jnp.exp(scores - log_total[:, None])
        grad_probs = jnp.dot(cotan_head, value_cols.T, preferred_element_type=jnp.float32)
        delta = jnp.sum(probs * grad_probs, axis=1)
        grad_scores = (probs * (grad_probs - delta[:, None])).astype(jnp.bfloat16)
        probs_low = probs.astype(jnp.bfloat16)
        query_head_grad = (score_scale * jnp.dot(grad_scores, latent_cache, preferred_element_type=jnp.float32)).astype(jnp.bfloat16)
        key_term = score_scale * jnp.dot(grad_scores.T, query_head, preferred_element_type=jnp.float32)
        value_term = jnp.dot(probs_low.T, cotan_head, preferred_element_type=jnp.float32)
        value_term = jnp.pad(value_term, ((0, 0), (0, ROPE)))
        return grad_total + key_term + value_term, query_head_grad

    start_grad = jnp.zeros((SEQ, LATENT + ROPE), jnp.float32)
    cache_grad, stacked = lax.scan(one_head, start_grad, jnp.arange(HEADS, dtype=jnp.int32))
    query_grad = jnp.transpose(stacked, (1, 0, 2))
    return query_grad, cache_grad
```

```python
import functools

import jax
import jax.numpy as jnp
from jax import lax
from jax.experimental import pallas as pl
from jax.experimental.pallas import tpu as pltpu
from jax.sharding import PartitionSpec as P

ROPE = 64
NOPE = 128
LATENT = 512
WIDTH = LATENT + ROPE
SCALE = (NOPE + ROPE) ** (-0.5)
MESH = pl.DeviceIdType.MESH
MASKED = -1e30
HOPS = (0, 2, -2, 4, -4, 6, -6, 8)


def kernel(
    start_ref, query_ref, cotan_ref, cache_ref,
    dq_ref, dc_ref,
    rows_q, rows_g, keys, probs, gprobs, dkeys, stats, norm,
    dq_part, dq_core, dq_out, dq_in, x_out, x_in, z_out, z_in,
    s_rows, r_q, r_g, s_key, r_zkey, s_fwd, r_xkey, s_stat, r_stat,
    s_core, r_core, s_dq, r_dq, s_x, r_x, s_z, r_z, s_fin, r_fin,
):
    ctx = lax.axis_index("ctx")
    tp = lax.axis_index("tp")
    xl, z = ctx // 16, ctx % 16
    xh, y, k = tp // 8, (tp // 2) % 4, tp % 2
    g = y * 2 + k
    parity = lax.rem(z + xh, 2)

    def dev(xl_=xl, z_=z, xh_=xh, y_=y, k_=k):
        return (xl_ * 16 + z_, (xh_ * 4 + y_) * 2 + k_)

    def remote(src, dst, ss, rs, to):
        return pltpu.make_async_remote_copy(
            src_ref=src, dst_ref=dst, send_sem=ss, recv_sem=rs, device_id=to, device_id_type=MESH
        )

    def ymod(s):
        return lax.rem(y + s, 4)

    def zmod(s):
        return lax.rem(z + s + 32, 16)

    x = xh * 2 + xl

    def xmod(s):
        x_ = lax.rem(x + s, 4)
        return x_ // 2, x_ % 2

    barrier = pltpu.get_barrier_semaphore()
    partners = []
    for s in range(1, 16):
        partners.append(dev(z_=zmod(s)))
    for s in (1, 3):
        hi, lo = xmod(s)
        partners.append(dev(xh_=hi, xl_=lo))
    for h in range(2):
        for s in range(4):
            for c in range(2):
                if h or s or c:
                    partners.append(dev(xh_=xh if h == 0 else 1 - xh, y_=ymod(s), k_=k if c == 0 else 1 - k))
    for p in partners:
        pl.semaphore_signal(barrier, inc=1, device_id=p, device_id_type=MESH)

    rows_q[pl.ds(pl.multiple_of(g * 128, 128), 128), :] = query_ref[...]
    rows_g[pl.ds(pl.multiple_of(g * 128, 128), 128), :] = cotan_ref[...]

    pl.semaphore_wait(barrier, len(partners))

    def rslot(ref, i):
        return ref.at[pl.ds(pl.multiple_of(i * 128, 128), 128), :]

    def kslot(ref, i):
        return ref.at[pl.ds(pl.multiple_of(i * 16, 16), 16), :]

    def block_slot(lo, zz):
        return (lo * 2 + lax.rem(zz, 2)) * 8 + zz // 2

    own_piece = kslot(cache_ref, g)

    def send_key(s):
        return remote(own_piece, kslot(keys, block_slot(xl, z)), s_key.at[s], r_zkey.at[z // 2], dev(z_=zmod(s)))

    order = (8, 7, 9, 6, 10, 5, 11, 4, 12, 3, 13, 2, 14, 1, 15)

    @pl.when(parity == 0)
    def _():
        for s in order:
            send_key(s).start()
        keys[pl.ds(pl.multiple_of(block_slot(xl, z) * 16, 16), 16), :] = cache_ref[
            pl.ds(pl.multiple_of(g * 16, 16), 16), :
        ]

    row_sends = []

    def send_rows(slot, to, i):
        for src, sems in ((rows_q, r_q), (rows_g, r_g)):
            c = remote(rslot(src, slot), rslot(src, slot), s_rows.at[i, 0 if src is rows_q else 1], sems.at[slot], to)
            c.start()
            row_sends.append(c)

    for i, s in enumerate((1, 3, 2)):
        send_rows(g, dev(y_=ymod(s)), i)
    send_rows(g, dev(k_=1 - k), 3)

    def wait_rows(slot):
        for src, sems in ((rows_q, r_q), (rows_g, r_g)):
            remote(rslot(src, slot), rslot(src, slot), s_rows.at[0, 0], sems.at[slot], dev(k_=1 - k)).wait_recv()

    def forward(slot, j, i, s):
        hi, lo = xmod(s)
        return remote(kslot(keys, slot), kslot(keys, slot), s_fwd.at[j, i], r_xkey.at[slot], dev(xh_=hi, xl_=lo))

    for j, hop in enumerate(HOPS):
        zz = zmod(hop - parity)
        slot = block_slot(xl, zz)

        def arrived():
            remote(own_piece, kslot(keys, slot), s_key.at[1], r_zkey.at[zz // 2], dev(z_=zmod(1))).wait_recv()

        if hop == 0:
            pl.when(parity == 1)(arrived)
        else:
            arrived()
        for i, s in enumerate((2, 1, 3)):
            forward(slot, j, i, s).start()

    for i, s in enumerate((1, 3, 2)):
        slot = ymod(s) * 2 + k
        wait_rows(slot)
        send_rows(slot, dev(k_=1 - k), 4 + i)

    for s in (1, 3, 2):
        hi, lo = xmod(s)
        for j in range(8):
            slot = (lo * 2 + hi) * 8 + j
            remote(own_piece, kslot(keys, slot), s_key.at[1], r_xkey.at[slot], dev(z_=zmod(1))).wait_recv()

    start = start_ref[0]
    n = lax.broadcasted_iota(jnp.int32, (512, 1), 0)
    group = n >> 7
    key_pos = (group >> 1) * 2048 + (((n >> 4) & 7) * 2 + (group & 1)) * 128 + g * 16 + (n & 15)
    row_pos = start + ((lax.broadcasted_iota(jnp.int32, (1, 256), 1) & 127) >> 3)
    nt = (((1,), (1,)), ((), ()))
    tn = (((0,), (0,)), ((), ()))

    for s in (0, 1, 3, 2):
        yy = ymod(s)
        wait_rows(yy * 2 + 1 - k)
        rows = pl.ds(pl.multiple_of(yy * 256, 256), 256)
        raw = lax.dot_general(keys[...], rows_q[rows, :], nt, preferred_element_type=jnp.float32) * SCALE
        scores = jnp.where(key_pos <= row_pos, raw, MASKED)
        gp = lax.dot_general(keys[:, :LATENT], rows_g[rows, :], nt, preferred_element_type=jnp.float32)
        top = jnp.max(scores, axis=0, keepdims=True)
        e = jnp.exp(scores - top)
        total = jnp.sum(e, axis=0, keepdims=True)
        dot = jnp.sum(e * gp, axis=0, keepdims=True)
        probs[yy] = e
        gprobs[yy] = gp
        for half in range(2):
            cols = slice(half * 128, half * 128 + 128)
            stats[g, 0, pl.ds(yy * 2 + half, 1), :] = top[:, cols]
            stats[g, 1, pl.ds(yy * 2 + half, 1), :] = total[:, cols]
            stats[g, 2, pl.ds(yy * 2 + half, 1), :] = dot[:, cols]

    stat_sends = []
    for s in range(4):
        for c in range(2):
            if s or c:
                copy = remote(
                    stats.at[g], stats.at[g], s_stat.at[s * 2 + c], r_stat.at[g],
                    dev(y_=ymod(s), k_=k if c == 0 else 1 - k),
                )
                copy.start()
                stat_sends.append(copy)
    for s in range(4):
        for c in range(2):
            if s or c:
                other = ymod(s) * 2 + (k if c == 0 else 1 - k)
                remote(stats.at[g], stats.at[other], s_stat.at[1], r_stat.at[other], dev(k_=1 - k)).wait_recv()

    tops = [stats[i, 0] for i in range(8)]
    top = functools.reduce(jnp.maximum, tops)
    weights = [jnp.exp(t - top) for t in tops]
    total = sum(w * stats[i, 1] for i, w in enumerate(weights))
    delta = sum(w * stats[i, 2] for i, w in enumerate(weights)) / total
    own_top = stats[g, 0]
    factor = jnp.exp(own_top - top) / total
    norm[0] = factor
    norm[1] = delta

    core_sends = []
    for at, s in enumerate((1, 3, 2, 0)):
        yy = ymod(s)
        rows = pl.ds(pl.multiple_of(yy * 256, 256), 256)
        f = jnp.concatenate([norm[0, pl.ds(yy * 2 + h, 1), :] for h in range(2)], axis=1)
        d = jnp.concatenate([norm[1, pl.ds(yy * 2 + h, 1), :] for h in range(2)], axis=1)
        p = probs[yy] * f
        gs = (p * (gprobs[yy] - d)).astype(jnp.bfloat16)
        low = p.astype(jnp.bfloat16)
        key_term = SCALE * jnp.dot(gs, rows_q[rows, :], preferred_element_type=jnp.float32)
        value_term = jnp.dot(low, rows_g[rows, :], preferred_element_type=jnp.float32)
        if at == 0:
            dkeys[...] = key_term
        else:
            dkeys[...] += key_term
        dkeys[:, :LATENT] += value_term
        part = lax.dot_general(gs, keys[...], tn, preferred_element_type=jnp.float32) * SCALE
        dq_part[at] = part.reshape(2, 128, WIDTH)
        copy = remote(dq_part.at[at, 1 - k], dq_core.at[at], s_core.at[at], r_core.at[at], dev(k_=1 - k))
        copy.start()
        core_sends.append(copy)

    x_sends = []
    for i, s in enumerate((2, 1, 3)):
        hi, lo = xmod(s)
        x_out[i] = dkeys[pl.ds(pl.multiple_of((lo * 2 + hi) * 128, 128), 128), :].astype(jnp.bfloat16)
        copy = remote(x_out.at[i], x_in.at[i], s_x.at[i], r_x.at[i], dev(xh_=hi, xl_=lo))
        copy.start()
        x_sends.append(copy)

    dq_sends = []
    for at, s in enumerate((1, 3, 2)):
        core_sends[at].wait_recv()
        dq_out[at] = dq_part[at, k] + dq_core[at]
        copy = remote(dq_out.at[at], dq_in.at[at], s_dq.at[at], r_dq.at[at], dev(y_=ymod(s)))
        copy.start()
        dq_sends.append(copy)
    core_sends[3].wait_recv()

    for copy in x_sends:
        copy.wait_recv()
    mine = dkeys[pl.ds(pl.multiple_of((xl * 2 + xh) * 128, 128), 128), :]
    for i in range(3):
        mine = mine + x_in[i].astype(jnp.float32)
    dkeys[pl.ds(0, 128), :] = mine
    z_out[...] = mine.astype(jnp.bfloat16)

    def z_send(j, hop):
        zz = zmod(hop - parity)
        return remote(kslot(z_out, zz // 2), z_in.at[z], s_z.at[j], r_z.at[z], dev(z_=zz))

    for j in reversed(range(8)):
        if HOPS[j] == 0:
            pl.when(parity == 1)(lambda: z_send(0, 0).start())
        else:
            z_send(j, HOPS[j]).start()

    dq = dq_part[3, k] + dq_core[3]
    for copy in dq_sends:
        copy.wait_recv()
    for at in range(3):
        dq = dq + dq_in[at]
    dq_ref[...] = dq.astype(jnp.bfloat16)

    fin = []
    for h in range(2):
        for s in range(4):
            for c in range(2):
                if h or s or c:
                    fin.append(dev(xh_=xh if h == 0 else 1 - xh, y_=ymod(s), k_=k if c == 0 else 1 - k))

    def fin_send(i):
        return remote(kslot(dc_ref, g), kslot(dc_ref, g), s_fin.at[i], r_fin.at[g], fin[i])

    @pl.when(parity == 0)
    def _():
        acc = dkeys[pl.ds(pl.multiple_of((z // 2) * 16, 16), 16), :]
        for s in range(1, 16):
            zz = zmod(s)
            remote(kslot(z_out, 0), z_in.at[zz], s_z.at[0], r_z.at[zz], dev(z_=zz)).wait_recv()
            acc = acc + z_in[zz].astype(jnp.float32)
        dc_ref[pl.ds(pl.multiple_of(g * 16, 16), 16), :] = acc
        for i in range(15):
            fin_send(i).start()
        for i in range(15):
            fin_send(i).wait_send()
        for s in order:
            send_key(s).wait_send()

    for s in range(4):
        for c in range(2):
            other = ymod(s) * 2 + (k if c == 0 else 1 - k)

            def wait_fin():
                remote(kslot(dc_ref, other), kslot(dc_ref, other), s_fin.at[0], r_fin.at[other], dev(k_=1 - k)).wait_recv()

            if s or c:
                wait_fin()
            else:
                pl.when(parity == 1)(wait_fin)

    for copy in row_sends + stat_sends + core_sends + x_sends + dq_sends:
        copy.wait_send()
    for j, hop in enumerate(HOPS):
        zz = zmod(hop - parity)
        slot = block_slot(xl, zz)
        for i, s in enumerate((2, 1, 3)):
            forward(slot, j, i, s).wait_send()
        if hop == 0:
            pl.when(parity == 1)(lambda: z_send(0, 0).wait_send())
        else:
            z_send(j, hop).wait_send()


def on_device(queries, grad_out, latent_cache, slab_starts):
    f32, bf16 = jnp.float32, jnp.bfloat16
    dma = pltpu.SemaphoreType.DMA
    vmem = pl.BlockSpec(memory_space=pltpu.VMEM)
    query_grad, cache_grad = pl.pallas_call(
        kernel,
        out_shape=(
            jax.ShapeDtypeStruct((128, WIDTH), bf16),
            jax.ShapeDtypeStruct((128, WIDTH), f32),
        ),
        in_specs=[pl.BlockSpec(memory_space=pltpu.SMEM), vmem, vmem, vmem],
        out_specs=[vmem, vmem],
        scratch_shapes=[
            pltpu.VMEM((1024, WIDTH), bf16),
            pltpu.VMEM((1024, LATENT), bf16),
            pltpu.VMEM((512, WIDTH), bf16),
            pltpu.VMEM((4, 512, 256), f32),
            pltpu.VMEM((4, 512, 256), f32),
            pltpu.VMEM((512, WIDTH), f32),
            pltpu.VMEM((8, 3, 8, 128), f32),
            pltpu.VMEM((2, 8, 128), f32),
            pltpu.VMEM((4, 2, 128, WIDTH), f32),
            pltpu.VMEM((4, 128, WIDTH), f32),
            pltpu.VMEM((3, 128, WIDTH), f32),
            pltpu.VMEM((3, 128, WIDTH), f32),
            pltpu.VMEM((3, 128, WIDTH), bf16),
            pltpu.VMEM((3, 128, WIDTH), bf16),
            pltpu.VMEM((128, WIDTH), bf16),
            pltpu.VMEM((16, 16, WIDTH), bf16),
            dma((7, 2)), dma((8,)), dma((8,)),
            dma((16,)), dma((8,)), dma((8, 3)), dma((32,)),
            dma((8,)), dma((8,)),
            dma((4,)), dma((4,)), dma((3,)), dma((3,)),
            dma((3,)), dma((3,)), dma((8,)), dma((16,)),
            dma((15,)), dma((8,)),
        ],
        compiler_params=pltpu.CompilerParams(
            collective_id=0, has_side_effects=True, vmem_limit_bytes=40 << 20
        ),
        cost_estimate=pl.CostEstimate(flops=2886000000, bytes_accessed=900000, transcendentals=530000),
        name="latent_attention_backward",
    )(
        slab_starts,
        queries.reshape(128, WIDTH),
        grad_out.reshape(128, LATENT),
        latent_cache,
    )
    return query_grad.reshape(queries.shape), cache_grad


def solution(mesh):
    placed = (P("ctx", "tp", None), P("ctx", "tp", None), P("ctx", None), P("ctx"))
    return jax.shard_map(
        on_device,
        mesh=mesh,
        in_specs=placed,
        out_specs=(P("ctx", "tp", None), P("ctx", None)),
        check_vma=False,
    )
```

```python
import functools

import jax
import jax.numpy as jnp
from jax import lax
from jax.experimental import pallas as pl
from jax.experimental.pallas import tpu as pltpu
from jax.sharding import PartitionSpec as P

ROPE = 64
NOPE = 128
LATENT = 512
WIDTH = LATENT + ROPE
SCALE = (NOPE + ROPE) ** (-0.5)
MESH = pl.DeviceIdType.MESH
MASKED = -1e30
HOPS = (6, 8, 10, 12, -2, 0, 2, 4)
OWN = 5
ARRIVE = (5, 6, 4, 7, 3, 0, 2, 1)
FAR = (8, 7, 9, 6, 10, 5, 11, 4, 12, 3, 13, 2, 14, 1, 15)
NEAR = FAR[::-1]


def kernel(
    start_ref, query_ref, cotan_ref, cache_ref,
    dq_ref, dc_ref,
    rows_q, rows_g, keys, probs, gprobs, gscores, plow, dkeys, stats,
    dq_part, dq_core, dq_out, dq_in, x_out, x_in, z_out, z_in, done,
    s_rows, r_q, r_g, s_key, r_zkey, s_fwd, r_xkey, s_stat, r_stat,
    s_core, r_core, s_dq, r_dq, s_x, r_x, s_z, r_z, s_fin, r_fin,
):
    ctx = lax.axis_index("ctx")
    tp = lax.axis_index("tp")
    xl, z = ctx // 16, ctx % 16
    xh, y, k = tp // 8, (tp // 2) % 4, tp % 2
    x = xh * 2 + xl
    g = y * 2 + k
    parity = lax.rem(z + xh, 2)

    def dev(xl_=xl, z_=z, xh_=xh, y_=y, k_=k):
        return (xl_ * 16 + z_, (xh_ * 4 + y_) * 2 + k_)

    def remote(src, dst, ss, rs, to):
        return pltpu.make_async_remote_copy(
            src_ref=src, dst_ref=dst, send_sem=ss, recv_sem=rs, device_id=to, device_id_type=MESH
        )

    def ymod(s):
        return lax.rem(y + s, 4)

    def zmod(s):
        return lax.rem(z + s + 32, 16)

    def xdev(s):
        x_ = lax.rem(x + s, 4)
        return dev(xh_=x_ // 2, xl_=x_ % 2)

    core = dev(k_=1 - k)

    barrier = pltpu.get_barrier_semaphore()
    partners = [dev(z_=zmod(s)) for s in FAR]
    partners += [xdev(1), xdev(3)]
    for h in range(2):
        for s in range(4):
            for c in range(2):
                if h or s or c:
                    partners.append(dev(xh_=xh if h == 0 else 1 - xh, y_=ymod(s), k_=k if c == 0 else 1 - k))
    for p in partners:
        pl.semaphore_signal(barrier, inc=1, device_id=p, device_id_type=MESH)

    def rslot(ref, i):
        return ref.at[pl.ds(pl.multiple_of(i * 128, 128), 128), :]

    def kslot(ref, i):
        return ref.at[pl.ds(pl.multiple_of(i * 16, 16), 16), :]

    own_rows = pl.ds(pl.multiple_of(g * 128, 128), 128)
    rows_q[own_rows, :] = query_ref[...]
    rows_g[own_rows, :] = cotan_ref[...]

    pl.semaphore_wait(barrier, len(partners))

    own_piece = kslot(cache_ref, g)

    def key_slot(r, j):
        return (j // 4) * 16 + ((r if j >= 4 else r + 3) % 4) * 4 + j % 4

    def send_key(s):
        j = next(j for j in range(8) if (HOPS[j] - s % 2 + s) % 16 == 0)
        return remote(own_piece, kslot(keys, key_slot(0, j)), s_key.at[s], r_zkey.at[j], dev(z_=zmod(s)))

    @pl.when(parity == 0)
    def _():
        for s in NEAR:
            send_key(s).start()
        keys[key_slot(0, OWN) * 16 : key_slot(0, OWN) * 16 + 16, :] = cache_ref[
            pl.ds(pl.multiple_of(g * 16, 16), 16), :
        ]

    row_sends = []

    def send_rows(n, slot, to):
        src, sems = ((rows_q, r_q), (rows_g, r_g))[n]
        c = remote(rslot(src, slot), rslot(src, slot), s_rows.at[len(row_sends)], sems.at[slot], to)
        c.start()
        row_sends.append(c)

    def wait_rows(n, slot):
        src, sems = ((rows_q, r_q), (rows_g, r_g))[n]
        remote(rslot(src, slot), rslot(src, slot), s_rows.at[0], sems.at[slot], core).wait_recv()

    right, left = dev(y_=ymod(1)), dev(y_=ymod(3))
    send_rows(0, g, right)
    send_rows(1, g, left)
    send_rows(1, g, right)
    send_rows(0, g, left)
    send_rows(0, g, core)
    send_rows(1, g, core)

    def forward(j, s):
        return remote(
            kslot(keys, key_slot(0, j)), kslot(keys, key_slot(4 - s, j)),
            s_fwd.at[j, s - 1], r_xkey.at[4 - s, j], xdev(s),
        )

    def pass_on(j):
        def arrived():
            remote(own_piece, kslot(keys, key_slot(0, j)), s_key.at[1], r_zkey.at[j], core).wait_recv()

        if j == OWN:
            pl.when(parity == 1)(arrived)
        else:
            arrived()
        for s in (2, 1, 3):
            forward(j, s).start()

    def pass_rows(s, n, ring):
        slot = ymod(s) * 2 + k
        wait_rows(n, slot)
        if ring is not None:
            send_rows(n, slot, ring)
        send_rows(n, slot, core)

    for j in ARRIVE[:4]:
        pass_on(j)
    pass_rows(3, 0, right)
    pass_rows(1, 1, left)
    for j in ARRIVE[4:6]:
        pass_on(j)
    pass_rows(3, 1, None)
    pass_rows(1, 0, None)
    for j in ARRIVE[6:]:
        pass_on(j)
    pass_rows(2, 0, None)
    pass_rows(2, 1, None)
    for n in range(2):
        wait_rows(n, g + 1 - 2 * k)

    nt = (((1,), (1,)), ((), ()))
    tn = (((0,), (0,)), ((), ()))
    row_pos = start_ref[0] + ((lax.broadcasted_iota(jnp.int32, (1, 256), 1) & 127) >> 3)

    def products(first, size, b):
        span = slice(first, first + size)
        n = first + lax.broadcasted_iota(jnp.int32, (size, 1), 0)
        half = n >> 8
        chip = (x + (n >> 6) + 1 - half) & 3
        hop = ((n >> 4) & 3) * 2 + 6 - 8 * half
        z_key = (z + hop - ((z + (chip >> 1)) & 1)) & 15
        key_pos = ((chip & 1) * 16 + z_key) * 128 + g * 16 + (n & 15)
        rows = pl.ds(pl.multiple_of(b * 256, 256), 256)
        raw = lax.dot_general(keys[span, :], rows_q[rows, :], nt, preferred_element_type=jnp.float32) * SCALE
        gp = lax.dot_general(keys[span, :LATENT], rows_g[rows, :], nt, preferred_element_type=jnp.float32)
        return jnp.where(key_pos <= row_pos, raw, MASKED), gp

    def keep_products(first, size, b):
        span = slice(first, first + size)
        scores, gp = products(first, size, b)
        probs[b, span, :] = scores
        gprobs[b, span, :] = gp

    for s in (0, 1, 3, 2):
        if s:
            for n in range(2):
                wait_rows(n, ymod(s) * 2 + 1 - k)
        keep_products(192, 128, ymod(s))

    def wait_keys(places):
        for j in places:
            for r in (1, 3, 2):
                slot = kslot(keys, key_slot(r, j))
                remote(own_piece, slot, s_key.at[1], r_xkey.at[r, j], core).wait_recv()

    wait_keys(ARRIVE[:4])
    for b in range(4):
        keep_products(320, 192, b)
    wait_keys(ARRIVE[4:])

    stat_sends = []
    for b in range(4):
        low, low_gp = products(0, 192, b)
        rest = probs[b, 192:, :]
        top = jnp.max(low, axis=0, keepdims=True)
        top = jnp.maximum(top, jnp.max(rest, axis=0, keepdims=True))
        total = dot = 0.0
        for span, part, gp in ((slice(0, 192), low, low_gp), (slice(192, 512), rest, gprobs[b, 192:, :])):
            e = jnp.exp(part - top)
            total = total + jnp.sum(e, axis=0, keepdims=True)
            dot = dot + jnp.sum(e * gp, axis=0, keepdims=True)
            probs[b, span, :] = e
        gprobs[b, :192, :] = low_gp
        for i, v in enumerate((top, total, dot)):
            for h in range(2):
                stats[g, b // 2, pl.ds(i * 4 + (b % 2) * 2 + h, 1), :] = v[:, h * 128 : h * 128 + 128]
        if b % 2:
            half = stats.at[g, b // 2]
            for s in (2, 1, 3, 0):
                for c in range(2):
                    if s or c:
                        copy = remote(
                            half, half, s_stat.at[b // 2, s * 2 + c], r_stat.at[b // 2, g],
                            dev(y_=ymod(s), k_=k if c == 0 else 1 - k),
                        )
                        copy.start()
                        stat_sends.append(copy)

    def normalize(half):
        for s in range(4):
            for c in range(2):
                if s or c:
                    other = ymod(s) * 2 + (k if c == 0 else 1 - k)
                    at = stats.at[other, half]
                    remote(at, at, s_stat.at[0, 0], r_stat.at[half, other], core).wait_recv()
        tops = [stats[i, half, :4, :] for i in range(8)]
        top = functools.reduce(jnp.maximum, tops)
        weights = [jnp.exp(t - top) for t in tops]
        total = sum(w * stats[i, half, 4:8, :] for i, w in enumerate(weights))
        delta = sum(w * stats[i, half, 8:12, :] for i, w in enumerate(weights)) / total
        factor = jnp.exp(stats[g, half, :4, :] - top) / total
        flat = lambda v: [jnp.concatenate([v[2 * i : 2 * i + 1], v[2 * i + 1 : 2 * i + 2]], axis=1) for i in range(2)]
        return flat(factor), flat(delta)

    def second(span, half, factor, delta):
        for i in range(2):
            b = half * 2 + i
            cols = slice(b * 256, b * 256 + 256)
            p = probs[b, span, :] * factor[i]
            gscores[span, cols] = (p * (gprobs[b, span, :] - delta[i])).astype(jnp.bfloat16)
            plow[span, cols] = p.astype(jnp.bfloat16)
        rows = slice(half * 512, half * 512 + 512)
        key_term = SCALE * jnp.dot(gscores[span, rows], rows_q[rows, :], preferred_element_type=jnp.float32)
        value_term = jnp.dot(plow[span, rows], rows_g[rows, :], preferred_element_type=jnp.float32)
        if half == 0:
            dkeys[span, :] = key_term
        else:
            dkeys[span, :] += key_term
        dkeys[span, :LATENT] += value_term

    factor, delta = normalize(0)
    second(slice(0, 512), 0, factor, delta)
    factor, delta = normalize(1)
    x_sends = []
    for half in range(2):
        second(slice(half * 256, half * 256 + 256), 1, factor, delta)
        for s in (2, 1, 3):
            at = key_slot(s, half * 4) * 16
            x_out[s - 1, half] = dkeys[at : at + 64, :].astype(jnp.bfloat16)
            copy = remote(
                x_out.at[s - 1, half], x_in.at[s - 1, half], s_x.at[s - 1, half], r_x.at[s - 1, half], xdev(s)
            )
            copy.start()
            x_sends.append(copy)

    core_sends = []
    hops_y = (2, 1, 3, 0)

    def query_part(at):
        cols = pl.ds(pl.multiple_of(ymod(hops_y[at]) * 256, 256), 256)
        part = lax.dot_general(gscores[:, cols], keys[...], tn, preferred_element_type=jnp.float32) * SCALE
        dq_part[at] = part.reshape(2, 128, WIDTH)
        copy = remote(dq_part.at[at, 1 - k], dq_core.at[at], s_core.at[at], r_core.at[at], core)
        copy.start()
        core_sends.append(copy)

    def z_send(j):
        return remote(kslot(z_out, j), z_in.at[z], s_z.at[j], r_z.at[z], dev(z_=zmod(HOPS[j] - parity)))

    def sum_x(half):
        at = key_slot(0, half * 4) * 16
        mine = dkeys[at : at + 64, :]
        for i, s in enumerate((2, 1, 3)):
            x_sends[half * 3 + i].wait_recv()
            mine = mine + x_in[s - 1, half].astype(jnp.float32)
        dkeys[at : at + 64, :] = mine
        z_out[half * 64 : half * 64 + 64, :] = mine.astype(jnp.bfloat16)
        for j in ((1, 2, 0, 3), (7, 4, 6, 5))[half]:
            if j == OWN:
                pl.when(parity == 1)(lambda: z_send(OWN).start())
            else:
                z_send(j).start()

    for at in range(4):
        query_part(at)
    dq_sends = []
    for at, s in enumerate(hops_y[:3]):
        core_sends[at].wait_recv()
        dq_out[at] = (dq_part[at, k] + dq_core[at]).astype(jnp.bfloat16)
        copy = remote(dq_out.at[at], dq_in.at[at], s_dq.at[at], r_dq.at[at], dev(y_=ymod(s)))
        copy.start()
        dq_sends.append(copy)
    sum_x(0)
    sum_x(1)

    fin = [dev(xh_=1 - xh, y_=ymod(s)) for s in (2, 1, 3, 0)] + [dev(y_=ymod(s)) for s in (2, 1, 3)]

    def fin_send(slot, i, to):
        return remote(kslot(done, slot), kslot(done, slot), s_fin.at[i], r_fin.at[slot], to)

    def wait_fin(slot):
        fin_send(slot, 0, core).wait_recv()

    @pl.when(parity == 0)
    def _():
        at = key_slot(0, OWN) * 16
        acc = dkeys[at : at + 16, :]
        for s in NEAR:
            zz = zmod(s)
            remote(kslot(z_out, 0), z_in.at[zz], s_z.at[0], r_z.at[zz], core).wait_recv()
            acc = acc + z_in[zz].astype(jnp.float32)
        done[pl.ds(pl.multiple_of(g * 16, 16), 16), :] = acc.astype(jnp.bfloat16)
        for i, to in enumerate(fin):
            fin_send(g, i, to).start()

    core_sends[3].wait_recv()
    dq = dq_part[3, k] + dq_core[3]
    for copy in dq_sends:
        copy.wait_recv()
    for at in range(3):
        dq = dq + dq_in[at].astype(jnp.float32)
    dq_ref[...] = dq.astype(jnp.bfloat16)

    for i, s in enumerate((0, 1, 3, 2)):
        slot = ymod(s) * 2 + k
        if s == 0:
            pl.when(parity == 1)(lambda: wait_fin(slot))
        else:
            wait_fin(slot)
        fin_send(slot, 7 + i, core).start()
    for s in (0, 1, 3, 2):
        wait_fin(ymod(s) * 2 + 1 - k)
    dc_ref[...] = done[...].astype(jnp.float32)

    @pl.when(parity == 0)
    def _():
        for s in FAR:
            send_key(s).wait_send()
        for i, to in enumerate(fin):
            fin_send(g, i, to).wait_send()

    for i in range(4):
        fin_send(g, 7 + i, core).wait_send()
    for copy in row_sends + stat_sends + core_sends + x_sends + dq_sends:
        copy.wait_send()
    for j in range(8):
        for s in (2, 1, 3):
            forward(j, s).wait_send()
        if j == OWN:
            pl.when(parity == 1)(lambda: z_send(OWN).wait_send())
        else:
            z_send(j).wait_send()


def on_device(queries, grad_out, latent_cache, slab_starts):
    f32, bf16 = jnp.float32, jnp.bfloat16
    dma = pltpu.SemaphoreType.DMA
    vmem = pl.BlockSpec(memory_space=pltpu.VMEM)
    query_grad, cache_grad = pl.pallas_call(
        kernel,
        out_shape=(
            jax.ShapeDtypeStruct((128, WIDTH), bf16),
            jax.ShapeDtypeStruct((128, WIDTH), f32),
        ),
        in_specs=[pl.BlockSpec(memory_space=pltpu.SMEM), vmem, vmem, vmem],
        out_specs=[vmem, vmem],
        scratch_shapes=[
            pltpu.VMEM((1024, WIDTH), bf16),
            pltpu.VMEM((1024, LATENT), bf16),
            pltpu.VMEM((512, WIDTH), bf16),
            pltpu.VMEM((4, 512, 256), f32),
            pltpu.VMEM((4, 512, 256), f32),
            pltpu.VMEM((512, 1024), bf16),
            pltpu.VMEM((512, 1024), bf16),
            pltpu.VMEM((512, WIDTH), f32),
            pltpu.VMEM((8, 2, 16, 128), f32),
            pltpu.VMEM((4, 2, 128, WIDTH), f32),
            pltpu.VMEM((4, 128, WIDTH), f32),
            pltpu.VMEM((3, 128, WIDTH), bf16),
            pltpu.VMEM((3, 128, WIDTH), bf16),
            pltpu.VMEM((3, 2, 64, WIDTH), bf16),
            pltpu.VMEM((3, 2, 64, WIDTH), bf16),
            pltpu.VMEM((128, WIDTH), bf16),
            pltpu.VMEM((16, 16, WIDTH), bf16),
            pltpu.VMEM((128, WIDTH), bf16),
            dma((14,)), dma((8,)), dma((8,)),
            dma((16,)), dma((8,)), dma((8, 3)), dma((4, 8)),
            dma((2, 8)), dma((2, 8)),
            dma((4,)), dma((4,)), dma((3,)), dma((3,)),
            dma((3, 2)), dma((3, 2)), dma((8,)), dma((16,)),
            dma((11,)), dma((8,)),
        ],
        compiler_params=pltpu.CompilerParams(
            collective_id=0, has_side_effects=True, vmem_limit_bytes=40 << 20
        ),
        cost_estimate=pl.CostEstimate(flops=2886000000, bytes_accessed=900000, transcendentals=530000),
        name="latent_attention_backward",
    )(
        slab_starts,
        queries.reshape(128, WIDTH),
        grad_out.reshape(128, LATENT),
        latent_cache,
    )
    return query_grad.reshape(queries.shape), cache_grad


def solution(mesh):
    placed = (P("ctx", "tp", None), P("ctx", "tp", None), P("ctx", None), P("ctx"))
    return jax.shard_map(
        on_device,
        mesh=mesh,
        in_specs=placed,
        out_specs=(P("ctx", "tp", None), P("ctx", None)),
        check_vma=False,
    )
```

```python
import functools

import jax
import jax.numpy as jnp
from jax import lax
from jax.experimental import pallas as pl
from jax.experimental.pallas import tpu as pltpu
from jax.sharding import PartitionSpec as P

ROPE = 64
NOPE = 128
LATENT = 512
WIDTH = LATENT + ROPE
SCALE = (NOPE + ROPE) ** (-0.5)
MESH = pl.DeviceIdType.MESH
MASKED = -1e30
HOPS = (6, 8, 10, 12, -2, 0, 2, 4)
OWN = 5
ARRIVE = (5, 6, 4, 7, 3, 0, 2, 1)
LEAVE = (1, 2, 0, 3, 7, 4, 6, 5)
FAR = (8, 7, 9, 6, 10, 5, 11, 4, 12, 3, 13, 2, 14, 1, 15)
NEAR = FAR[::-1]


def kernel(
    start_ref, query_ref, cotan_ref, cache_ref,
    dq_ref, dc_ref,
    rows_q, rows_g, keys, probs, gprobs, gscores, plow, dkeys, stats,
    dq_part, dq_core, dq_out, dq_in, x_out, x_in, z_out, z_in, done,
    s_rows, r_q, r_g, s_key, r_zkey, s_fwd, r_xkey, s_stat, r_stat,
    s_core, r_core, s_dq, r_dq, s_x, r_x, s_z, r_z, s_fin, r_fin,
):
    ctx = lax.axis_index("ctx")
    tp = lax.axis_index("tp")
    xl, z = ctx // 16, ctx % 16
    xh, y, k = tp // 8, (tp // 2) % 4, tp % 2
    x = xh * 2 + xl
    g = y * 2 + k
    parity = lax.rem(z + xh, 2)

    def dev(xl_=xl, z_=z, xh_=xh, y_=y, k_=k):
        return (xl_ * 16 + z_, (xh_ * 4 + y_) * 2 + k_)

    def remote(src, dst, ss, rs, to):
        return pltpu.make_async_remote_copy(
            src_ref=src, dst_ref=dst, send_sem=ss, recv_sem=rs, device_id=to, device_id_type=MESH
        )

    def ymod(s):
        return lax.rem(y + s, 4)

    def zmod(s):
        return lax.rem(z + s + 32, 16)

    def xdev(s):
        x_ = lax.rem(x + s, 4)
        return dev(xh_=x_ // 2, xl_=x_ % 2)

    core = dev(k_=1 - k)

    barrier = pltpu.get_barrier_semaphore()
    partners = [dev(z_=zmod(s)) for s in FAR]
    partners += [xdev(1), xdev(3)]
    for h in range(2):
        for s in range(4):
            for c in range(2):
                if (c == 0 and (h or s)) or (c and not h):
                    partners.append(dev(xh_=xh if h == 0 else 1 - xh, y_=ymod(s), k_=k if c == 0 else 1 - k))
    for p in partners:
        pl.semaphore_signal(barrier, inc=1, device_id=p, device_id_type=MESH)

    def rslot(ref, i):
        return ref.at[pl.ds(pl.multiple_of(i * 128, 128), 128), :]

    def kslot(ref, i):
        return ref.at[pl.ds(pl.multiple_of(i * 16, 16), 16), :]

    own_rows = pl.ds(pl.multiple_of(g * 128, 128), 128)
    rows_q[own_rows, :] = query_ref[...]
    rows_g[own_rows, :] = cotan_ref[...]

    pl.semaphore_wait(barrier, len(partners))

    own_piece = kslot(cache_ref, g)

    def key_slot(r, j):
        return (j // 4) * 16 + ((r if j >= 4 else r + 3) % 4) * 4 + j % 4

    def send_key(s):
        j = next(j for j in range(8) if (HOPS[j] - s % 2 + s) % 16 == 0)
        return remote(own_piece, kslot(keys, key_slot(0, j)), s_key.at[s], r_zkey.at[j], dev(z_=zmod(s)))

    @pl.when(parity == 0)
    def _():
        for s in NEAR:
            send_key(s).start()
        keys[key_slot(0, OWN) * 16 : key_slot(0, OWN) * 16 + 16, :] = cache_ref[
            pl.ds(pl.multiple_of(g * 16, 16), 16), :
        ]

    row_sends = []

    def send_rows(n, slot, to):
        src, sems = ((rows_q, r_q), (rows_g, r_g))[n]
        c = remote(rslot(src, slot), rslot(src, slot), s_rows.at[len(row_sends)], sems.at[slot], to)
        c.start()
        row_sends.append(c)

    def wait_rows(n, slot):
        src, sems = ((rows_q, r_q), (rows_g, r_g))[n]
        remote(rslot(src, slot), rslot(src, slot), s_rows.at[0], sems.at[slot], core).wait_recv()

    right, left = dev(y_=ymod(1)), dev(y_=ymod(3))
    send_rows(0, g, right)
    send_rows(1, g, left)
    send_rows(1, g, right)
    send_rows(0, g, left)
    send_rows(0, g, core)
    send_rows(1, g, core)

    def forward(j, s):
        return remote(
            kslot(keys, key_slot(0, j)), kslot(keys, key_slot(4 - s, j)),
            s_fwd.at[j, s - 1], r_xkey.at[4 - s, j], xdev(s),
        )

    def pass_on(j):
        def arrived():
            remote(own_piece, kslot(keys, key_slot(0, j)), s_key.at[1], r_zkey.at[j], core).wait_recv()

        if j == OWN:
            pl.when(parity == 1)(arrived)
        else:
            arrived()
        for s in (2, 1, 3):
            forward(j, s).start()

    def pass_rows(s, n, ring):
        slot = ymod(s) * 2 + k
        wait_rows(n, slot)
        if ring is not None:
            send_rows(n, slot, ring)
        send_rows(n, slot, core)

    for j in ARRIVE[:4]:
        pass_on(j)
    pass_rows(3, 0, right)
    pass_rows(1, 1, left)
    for j in ARRIVE[4:6]:
        pass_on(j)
    pass_rows(3, 1, None)
    pass_rows(1, 0, None)
    for j in ARRIVE[6:]:
        pass_on(j)
    pass_rows(2, 0, None)
    pass_rows(2, 1, None)
    for n in range(2):
        wait_rows(n, g + 1 - 2 * k)

    nt = (((1,), (1,)), ((), ()))
    tn = (((0,), (0,)), ((), ()))
    row_pos = start_ref[0] + ((lax.broadcasted_iota(jnp.int32, (1, 256), 1) & 127) >> 3)

    def products(first, size, b):
        span = slice(first, first + size)
        n = first + lax.broadcasted_iota(jnp.int32, (size, 1), 0)
        half = n >> 8
        chip = (x + (n >> 6) + 1 - half) & 3
        hop = ((n >> 4) & 3) * 2 + 6 - 8 * half
        z_key = (z + hop - ((z + (chip >> 1)) & 1)) & 15
        key_pos = ((chip & 1) * 16 + z_key) * 128 + g * 16 + (n & 15)
        rows = pl.ds(pl.multiple_of(b * 256, 256), 256)
        raw = lax.dot_general(keys[span, :], rows_q[rows, :], nt, preferred_element_type=jnp.float32) * SCALE
        gp = lax.dot_general(keys[span, :LATENT], rows_g[rows, :], nt, preferred_element_type=jnp.float32)
        return jnp.where(key_pos <= row_pos, raw, MASKED), gp

    def keep_products(first, size, b):
        span = slice(first, first + size)
        scores, gp = products(first, size, b)
        probs[b, span, :] = scores
        gprobs[b, span, :] = gp

    for s in (0, 1, 3, 2):
        if s:
            for n in range(2):
                wait_rows(n, ymod(s) * 2 + 1 - k)
        keep_products(192, 128, ymod(s))

    def wait_keys(places):
        for j in places:
            for r in (1, 3, 2):
                slot = kslot(keys, key_slot(r, j))
                remote(own_piece, slot, s_key.at[1], r_xkey.at[r, j], core).wait_recv()

    def reduce_tile(span, b, scores, gp):
        top = jnp.max(scores, axis=0, keepdims=True)
        e = jnp.exp(scores - top)
        probs[b, span, :] = e
        return top, jnp.sum(e, axis=0, keepdims=True), jnp.sum(e * gp, axis=0, keepdims=True)

    wait_keys(ARRIVE[:4])
    rest = []
    for b in range(4):
        keep_products(320, 192, b)
        rest.append(reduce_tile(slice(192, 512), b, probs[b, 192:, :], gprobs[b, 192:, :]))
    wait_keys(ARRIVE[4:])

    stat_sends = []
    scales = []
    for b in range(4):
        scores, gp = products(0, 192, b)
        gprobs[b, :192, :] = gp
        top0, total0, dot0 = reduce_tile(slice(0, 192), b, scores, gp)
        top1, total1, dot1 = rest[b]
        top = jnp.maximum(top0, top1)
        w0, w1 = jnp.exp(top0 - top), jnp.exp(top1 - top)
        scales.append((w0, w1))
        total = total0 * w0 + total1 * w1
        dot = dot0 * w0 + dot1 * w1
        for i, v in enumerate((top, total, dot)):
            for h in range(2):
                stats[g, b // 2, pl.ds(i * 4 + (b % 2) * 2 + h, 1), :] = v[:, h * 128 : h * 128 + 128]
        if b % 2:
            half = stats.at[g, b // 2]
            for s in (2, 1, 3, 0):
                for c in range(2):
                    if s or c:
                        copy = remote(
                            half, half, s_stat.at[b // 2, s * 2 + c], r_stat.at[b // 2, g],
                            dev(y_=ymod(s), k_=k if c == 0 else 1 - k),
                        )
                        copy.start()
                        stat_sends.append(copy)

    def normalize(half):
        for s in range(4):
            for c in range(2):
                if s or c:
                    other = ymod(s) * 2 + (k if c == 0 else 1 - k)
                    at = stats.at[other, half]
                    remote(at, at, s_stat.at[0, 0], r_stat.at[half, other], core).wait_recv()
        tops = [stats[i, half, :4, :] for i in range(8)]
        top = functools.reduce(jnp.maximum, tops)
        weights = [jnp.exp(t - top) for t in tops]
        total = sum(w * stats[i, half, 4:8, :] for i, w in enumerate(weights))
        delta = sum(w * stats[i, half, 8:12, :] for i, w in enumerate(weights)) / total
        factor = jnp.exp(stats[g, half, :4, :] - top) / total
        flat = lambda v: [jnp.concatenate([v[2 * i : 2 * i + 1], v[2 * i + 1 : 2 * i + 2]], axis=1) for i in range(2)]
        return flat(factor), flat(delta)

    def second(span, half, factor, delta):
        for i in range(2):
            b = half * 2 + i
            cols = slice(b * 256, b * 256 + 256)
            for part, w in ((slice(span.start, min(span.stop, 192)), 0), (slice(max(span.start, 192), span.stop), 1)):
                if part.start < part.stop:
                    p = probs[b, part, :] * (factor[i] * scales[b][w])
                    gscores[part, cols] = (p * (gprobs[b, part, :] - delta[i])).astype(jnp.bfloat16)
                    plow[part, cols] = p.astype(jnp.bfloat16)
        rows = slice(half * 512, half * 512 + 512)
        key_term = SCALE * jnp.dot(gscores[span, rows], rows_q[rows, :], preferred_element_type=jnp.float32)
        value_term = jnp.dot(plow[span, rows], rows_g[rows, :], preferred_element_type=jnp.float32)
        if half == 0:
            dkeys[span, :] = key_term
        else:
            dkeys[span, :] += key_term
        dkeys[span, :LATENT] += value_term

    factor, delta = normalize(0)
    second(slice(0, 512), 0, factor, delta)
    factor, delta = normalize(1)

    def x_send(s, j):
        return remote(
            kslot(x_out.at[s - 1], j), kslot(x_in.at[s - 1], j), s_x.at[s - 1, j], r_x.at[s - 1, j], xdev(s)
        )

    for half in range(2):
        second(slice(half * 256, half * 256 + 256), 1, factor, delta)
        for s in (1, 2, 3):
            at = key_slot(s, half * 4) * 16
            x_out[s - 1, half * 64 : half * 64 + 64, :] = dkeys[at : at + 64, :].astype(jnp.bfloat16)
        for j in LEAVE[half * 4 : half * 4 + 4]:
            for s in (2, 1, 3):
                x_send(s, j).start()

    core_sends = []
    hops_y = (2, 1, 3, 0)

    def query_part(at):
        cols = pl.ds(pl.multiple_of(ymod(hops_y[at]) * 256, 256), 256)
        part = lax.dot_general(gscores[:, cols], keys[...], tn, preferred_element_type=jnp.float32) * SCALE
        dq_part[at] = part.reshape(2, 128, WIDTH)
        copy = remote(dq_part.at[at, 1 - k], dq_core.at[at], s_core.at[at], r_core.at[at], core)
        copy.start()
        core_sends.append(copy)

    def z_send(j):
        return remote(kslot(z_out, j), z_in.at[z], s_z.at[j], r_z.at[z], dev(z_=zmod(HOPS[j] - parity)))

    def sum_x(j):
        at = key_slot(0, j) * 16
        mine = dkeys[at : at + 16, :]
        for s in (1, 3, 2):
            x_send(s, j).wait_recv()
            mine = mine + x_in[s - 1, j * 16 : j * 16 + 16, :].astype(jnp.float32)
        dkeys[at : at + 16, :] = mine
        z_out[j * 16 : j * 16 + 16, :] = mine.astype(jnp.bfloat16)
        if j == OWN:
            pl.when(parity == 1)(lambda: z_send(OWN).start())
        else:
            z_send(j).start()

    for at in range(4):
        query_part(at)
    for j in LEAVE[:4]:
        sum_x(j)
    dq_sends = []
    for at, s in enumerate(hops_y[:3]):
        core_sends[at].wait_recv()
        dq_out[at] = (dq_part[at, k] + dq_core[at]).astype(jnp.bfloat16)
        copy = remote(dq_out.at[at], dq_in.at[at], s_dq.at[at], r_dq.at[at], dev(y_=ymod(s)))
        copy.start()
        dq_sends.append(copy)
    for j in LEAVE[4:]:
        sum_x(j)

    fin = [dev(xh_=1 - xh, y_=ymod(s)) for s in (2, 1, 3, 0)] + [dev(y_=ymod(s)) for s in (2, 1, 3)]

    def fin_send(slot, i, to):
        return remote(kslot(done, slot), kslot(done, slot), s_fin.at[i], r_fin.at[slot], to)

    def wait_fin(slot):
        fin_send(slot, 0, core).wait_recv()

    @pl.when(parity == 0)
    def _():
        at = key_slot(0, OWN) * 16
        acc = dkeys[at : at + 16, :]
        for s in NEAR:
            zz = zmod(s)
            remote(kslot(z_out, 0), z_in.at[zz], s_z.at[0], r_z.at[zz], core).wait_recv()
            acc = acc + z_in[zz].astype(jnp.float32)
        done[pl.ds(pl.multiple_of(g * 16, 16), 16), :] = acc.astype(jnp.bfloat16)
        for i, to in enumerate(fin):
            fin_send(g, i, to).start()

    core_sends[3].wait_recv()
    dq = dq_part[3, k] + dq_core[3]
    for copy in dq_sends:
        copy.wait_recv()
    for at in range(3):
        dq = dq + dq_in[at].astype(jnp.float32)
    dq_ref[...] = dq.astype(jnp.bfloat16)

    for i, s in enumerate((0, 1, 3, 2)):
        slot = ymod(s) * 2 + k
        if s == 0:
            pl.when(parity == 1)(lambda: wait_fin(slot))
        else:
            wait_fin(slot)
        fin_send(slot, 7 + i, core).start()
    for s in (0, 1, 3, 2):
        wait_fin(ymod(s) * 2 + 1 - k)
    dc_ref[...] = done[...].astype(jnp.float32)

    @pl.when(parity == 0)
    def _():
        for s in FAR:
            send_key(s).wait_send()
        for i, to in enumerate(fin):
            fin_send(g, i, to).wait_send()

    for i in range(4):
        fin_send(g, 7 + i, core).wait_send()
    for copy in row_sends + stat_sends + core_sends + dq_sends:
        copy.wait_send()
    for j in range(8):
        for s in (2, 1, 3):
            forward(j, s).wait_send()
            x_send(s, j).wait_send()
        if j == OWN:
            pl.when(parity == 1)(lambda: z_send(OWN).wait_send())
        else:
            z_send(j).wait_send()


def on_device(queries, grad_out, latent_cache, slab_starts):
    f32, bf16 = jnp.float32, jnp.bfloat16
    dma = pltpu.SemaphoreType.DMA
    vmem = pl.BlockSpec(memory_space=pltpu.VMEM)
    query_grad, cache_grad = pl.pallas_call(
        kernel,
        out_shape=(
            jax.ShapeDtypeStruct((128, WIDTH), bf16),
            jax.ShapeDtypeStruct((128, WIDTH), f32),
        ),
        in_specs=[pl.BlockSpec(memory_space=pltpu.SMEM), vmem, vmem, vmem],
        out_specs=[vmem, vmem],
        scratch_shapes=[
            pltpu.VMEM((1024, WIDTH), bf16),
            pltpu.VMEM((1024, LATENT), bf16),
            pltpu.VMEM((512, WIDTH), bf16),
            pltpu.VMEM((4, 512, 256), f32),
            pltpu.VMEM((4, 512, 256), f32),
            pltpu.VMEM((512, 1024), bf16),
            pltpu.VMEM((512, 1024), bf16),
            pltpu.VMEM((512, WIDTH), f32),
            pltpu.VMEM((8, 2, 16, 128), f32),
            pltpu.VMEM((4, 2, 128, WIDTH), f32),
            pltpu.VMEM((4, 128, WIDTH), f32),
            pltpu.VMEM((3, 128, WIDTH), bf16),
            pltpu.VMEM((3, 128, WIDTH), bf16),
            pltpu.VMEM((3, 128, WIDTH), bf16),
            pltpu.VMEM((3, 128, WIDTH), bf16),
            pltpu.VMEM((128, WIDTH), bf16),
            pltpu.VMEM((16, 16, WIDTH), bf16),
            pltpu.VMEM((128, WIDTH), bf16),
            dma((14,)), dma((8,)), dma((8,)),
            dma((16,)), dma((8,)), dma((8, 3)), dma((4, 8)),
            dma((2, 8)), dma((2, 8)),
            dma((4,)), dma((4,)), dma((3,)), dma((3,)),
            dma((3, 8)), dma((3, 8)), dma((8,)), dma((16,)),
            dma((11,)), dma((8,)),
        ],
        compiler_params=pltpu.CompilerParams(
            collective_id=0, has_side_effects=True, vmem_limit_bytes=40 << 20
        ),
        cost_estimate=pl.CostEstimate(flops=2886000000, bytes_accessed=900000, transcendentals=530000),
        name="latent_attention_backward",
    )(
        slab_starts,
        queries.reshape(128, WIDTH),
        grad_out.reshape(128, LATENT),
        latent_cache,
    )
    return query_grad.reshape(queries.shape), cache_grad


def solution(mesh):
    placed = (P("ctx", "tp", None), P("ctx", "tp", None), P("ctx", None), P("ctx"))
    return jax.shard_map(
        on_device,
        mesh=mesh,
        in_specs=placed,
        out_specs=(P("ctx", "tp", None), P("ctx", None)),
        check_vma=False,
    )
```

```python
import functools

import jax
import jax.numpy as jnp
from jax import lax
from jax.experimental import pallas as pl
from jax.experimental.pallas import tpu as pltpu
from jax.sharding import PartitionSpec as P

ROPE = 64
NOPE = 128
LATENT = 512
WIDTH = LATENT + ROPE
SCALE = (NOPE + ROPE) ** (-0.5)
MESH = pl.DeviceIdType.MESH
MASKED = -1e30
HOPS = (6, 8, 10, 12, -2, 0, 2, 4)
OWN = 5
ARRIVE = (5, 6, 4, 7, 3, 0, 2, 1)
LEAVE = (1, 2, 0, 3, 7, 4, 6, 5)
FAR = (8, 7, 9, 6, 10, 5, 11, 4, 12, 3, 13, 2, 14, 1, 15)
NEAR = FAR[::-1]


def kernel(
    start_ref, query_ref, cotan_ref, cache_ref,
    dq_ref, dc_ref,
    rows_q, rows_g, keys, probs, gprobs, gscores, plow, dkeys, stats,
    dq_part, dq_core, dq_out, dq_in, x_out, x_in, z_out, z_in,
    s_rows, r_q, r_g, s_key, r_zkey, s_fwd, r_xkey, s_stat, r_stat,
    s_core, r_core, s_dq, r_dq, s_x, r_x, s_z, r_z, s_fin, r_fin,
):
    ctx = lax.axis_index("ctx")
    tp = lax.axis_index("tp")
    xl, z = ctx // 16, ctx % 16
    xh, y, k = tp // 8, (tp // 2) % 4, tp % 2
    x = xh * 2 + xl
    g = y * 2 + k
    parity = lax.rem(z + xh, 2)

    def dev(xl_=xl, z_=z, xh_=xh, y_=y, k_=k):
        return (xl_ * 16 + z_, (xh_ * 4 + y_) * 2 + k_)

    def remote(src, dst, ss, rs, to):
        return pltpu.make_async_remote_copy(
            src_ref=src, dst_ref=dst, send_sem=ss, recv_sem=rs, device_id=to, device_id_type=MESH
        )

    def ymod(s):
        return lax.rem(y + s, 4)

    def zmod(s):
        return lax.rem(z + s + 32, 16)

    def xdev(s):
        x_ = lax.rem(x + s, 4)
        return dev(xh_=x_ // 2, xl_=x_ % 2)

    core = dev(k_=1 - k)

    barrier = pltpu.get_barrier_semaphore()
    partners = [dev(z_=zmod(s)) for s in FAR]
    partners += [xdev(1), xdev(3)]
    for h in range(2):
        for s in range(4):
            for c in range(2):
                if (c == 0 and (h or s)) or (c and not h):
                    partners.append(dev(xh_=xh if h == 0 else 1 - xh, y_=ymod(s), k_=k if c == 0 else 1 - k))
    for p in partners:
        pl.semaphore_signal(barrier, inc=1, device_id=p, device_id_type=MESH)

    def rslot(ref, i):
        return ref.at[pl.ds(pl.multiple_of(i * 128, 128), 128), :]

    def kslot(ref, i):
        return ref.at[pl.ds(pl.multiple_of(i * 16, 16), 16), :]

    own_rows = pl.ds(pl.multiple_of(g * 128, 128), 128)
    rows_q[own_rows, :] = query_ref[...]
    rows_g[own_rows, :] = cotan_ref[...]

    pl.semaphore_wait(barrier, len(partners))

    own_piece = kslot(cache_ref, g)

    def key_slot(r, j):
        return (j // 4) * 16 + ((r if j >= 4 else r + 3) % 4) * 4 + j % 4

    def send_key(s):
        j = next(j for j in range(8) if (HOPS[j] - s % 2 + s) % 16 == 0)
        return remote(own_piece, kslot(keys, key_slot(0, j)), s_key.at[s], r_zkey.at[j], dev(z_=zmod(s)))

    @pl.when(parity == 0)
    def _():
        for s in NEAR:
            send_key(s).start()
        keys[key_slot(0, OWN) * 16 : key_slot(0, OWN) * 16 + 16, :] = cache_ref[
            pl.ds(pl.multiple_of(g * 16, 16), 16), :
        ]

    row_sends = []

    def send_rows(n, slot, to):
        src, sems = ((rows_q, r_q), (rows_g, r_g))[n]
        c = remote(rslot(src, slot), rslot(src, slot), s_rows.at[len(row_sends)], sems.at[slot], to)
        c.start()
        row_sends.append(c)

    def wait_rows(n, slot):
        src, sems = ((rows_q, r_q), (rows_g, r_g))[n]
        remote(rslot(src, slot), rslot(src, slot), s_rows.at[0], sems.at[slot], core).wait_recv()

    right, left = dev(y_=ymod(1)), dev(y_=ymod(3))
    send_rows(0, g, right)
    send_rows(1, g, left)
    send_rows(1, g, right)
    send_rows(0, g, left)
    send_rows(0, g, core)
    send_rows(1, g, core)

    def forward(j, s):
        return remote(
            kslot(keys, key_slot(0, j)), kslot(keys, key_slot(4 - s, j)),
            s_fwd.at[j, s - 1], r_xkey.at[4 - s, j], xdev(s),
        )

    def pass_on(j):
        def arrived():
            remote(own_piece, kslot(keys, key_slot(0, j)), s_key.at[1], r_zkey.at[j], core).wait_recv()

        if j == OWN:
            pl.when(parity == 1)(arrived)
        else:
            arrived()
        for s in (2, 1, 3):
            forward(j, s).start()

    def pass_rows(s, n, ring):
        slot = ymod(s) * 2 + k
        wait_rows(n, slot)
        if ring is not None:
            send_rows(n, slot, ring)
        send_rows(n, slot, core)

    for j in ARRIVE[:4]:
        pass_on(j)
    pass_rows(3, 0, right)
    pass_rows(1, 1, left)
    for j in ARRIVE[4:6]:
        pass_on(j)
    pass_rows(3, 1, None)
    pass_rows(1, 0, None)
    for j in ARRIVE[6:]:
        pass_on(j)
    pass_rows(2, 0, None)
    pass_rows(2, 1, None)
    for n in range(2):
        wait_rows(n, g + 1 - 2 * k)

    nt = (((1,), (1,)), ((), ()))
    tn = (((0,), (0,)), ((), ()))
    row_pos = start_ref[0] + ((lax.broadcasted_iota(jnp.int32, (1, 256), 1) & 127) >> 3)

    def products(first, size, b):
        span = slice(first, first + size)
        n = first + lax.broadcasted_iota(jnp.int32, (size, 1), 0)
        half = n >> 8
        chip = (x + (n >> 6) + 1 - half) & 3
        hop = ((n >> 4) & 3) * 2 + 6 - 8 * half
        z_key = (z + hop - ((z + (chip >> 1)) & 1)) & 15
        key_pos = ((chip & 1) * 16 + z_key) * 128 + g * 16 + (n & 15)
        rows = pl.ds(pl.multiple_of(b * 256, 256), 256)
        raw = lax.dot_general(keys[span, :], rows_q[rows, :], nt, preferred_element_type=jnp.float32) * SCALE
        gp = lax.dot_general(keys[span, :LATENT], rows_g[rows, :], nt, preferred_element_type=jnp.float32)
        return jnp.where(key_pos <= row_pos, raw, MASKED), gp

    def keep_products(first, size, b):
        span = slice(first, first + size)
        scores, gp = products(first, size, b)
        probs[b, span, :] = scores
        gprobs[b, span, :] = gp

    for s in (0, 1, 3, 2):
        if s:
            for n in range(2):
                wait_rows(n, ymod(s) * 2 + 1 - k)
        keep_products(192, 128, ymod(s))

    def wait_keys(places):
        for j in places:
            for r in (1, 3, 2):
                slot = kslot(keys, key_slot(r, j))
                remote(own_piece, slot, s_key.at[1], r_xkey.at[r, j], core).wait_recv()

    def reduce_tile(span, b, scores, gp):
        top = jnp.max(scores, axis=0, keepdims=True)
        e = jnp.exp(scores - top)
        probs[b, span, :] = e
        return top, jnp.sum(e, axis=0, keepdims=True), jnp.sum(e * gp, axis=0, keepdims=True)

    wait_keys(ARRIVE[:4])
    rest = []
    for b in range(4):
        keep_products(320, 192, b)
        rest.append(reduce_tile(slice(192, 512), b, probs[b, 192:, :], gprobs[b, 192:, :]))
    wait_keys(ARRIVE[4:])

    stat_sends = []
    scales = []
    for b in range(4):
        scores, gp = products(0, 192, b)
        gprobs[b, :192, :] = gp
        top0, total0, dot0 = reduce_tile(slice(0, 192), b, scores, gp)
        top1, total1, dot1 = rest[b]
        top = jnp.maximum(top0, top1)
        w0, w1 = jnp.exp(top0 - top), jnp.exp(top1 - top)
        scales.append((w0, w1))
        total = total0 * w0 + total1 * w1
        dot = dot0 * w0 + dot1 * w1
        for i, v in enumerate((top, total, dot)):
            for h in range(2):
                stats[g, b // 2, pl.ds(i * 4 + (b % 2) * 2 + h, 1), :] = v[:, h * 128 : h * 128 + 128]
        if b % 2:
            half = stats.at[g, b // 2]
            for s in (2, 1, 3, 0):
                for c in range(2):
                    if s or c:
                        copy = remote(
                            half, half, s_stat.at[b // 2, s * 2 + c], r_stat.at[b // 2, g],
                            dev(y_=ymod(s), k_=k if c == 0 else 1 - k),
                        )
                        copy.start()
                        stat_sends.append(copy)

    def normalize(half):
        for s in range(4):
            for c in range(2):
                if s or c:
                    other = ymod(s) * 2 + (k if c == 0 else 1 - k)
                    at = stats.at[other, half]
                    remote(at, at, s_stat.at[0, 0], r_stat.at[half, other], core).wait_recv()
        tops = [stats[i, half, :4, :] for i in range(8)]
        top = functools.reduce(jnp.maximum, tops)
        weights = [jnp.exp(t - top) for t in tops]
        total = sum(w * stats[i, half, 4:8, :] for i, w in enumerate(weights))
        delta = sum(w * stats[i, half, 8:12, :] for i, w in enumerate(weights)) / total
        factor = jnp.exp(stats[g, half, :4, :] - top) / total
        flat = lambda v: [jnp.concatenate([v[2 * i : 2 * i + 1], v[2 * i + 1 : 2 * i + 2]], axis=1) for i in range(2)]
        return flat(factor), flat(delta)

    def second(span, half, factor, delta):
        for i in range(2):
            b = half * 2 + i
            cols = slice(b * 256, b * 256 + 256)
            for part, w in ((slice(span.start, min(span.stop, 192)), 0), (slice(max(span.start, 192), span.stop), 1)):
                if part.start < part.stop:
                    p = probs[b, part, :] * (factor[i] * scales[b][w])
                    gscores[part, cols] = (p * (gprobs[b, part, :] - delta[i])).astype(jnp.bfloat16)
                    plow[part, cols] = p.astype(jnp.bfloat16)
        rows = slice(half * 512, half * 512 + 512)
        key_term = SCALE * jnp.dot(gscores[span, rows], rows_q[rows, :], preferred_element_type=jnp.float32)
        value_term = jnp.dot(plow[span, rows], rows_g[rows, :], preferred_element_type=jnp.float32)
        if half == 0:
            dkeys[span, :] = key_term
        else:
            dkeys[span, :] += key_term
        dkeys[span, :LATENT] += value_term

    factor, delta = normalize(0)
    second(slice(0, 512), 0, factor, delta)
    factor, delta = normalize(1)

    def x_send(s, j):
        return remote(
            kslot(x_out.at[s - 1], j), kslot(x_in.at[s - 1], j), s_x.at[s - 1, j], r_x.at[s - 1, j], xdev(s)
        )

    for half in range(2):
        second(slice(half * 256, half * 256 + 256), 1, factor, delta)
        for s in (1, 2, 3):
            at = key_slot(s, half * 4) * 16
            x_out[s - 1, half * 64 : half * 64 + 64, :] = dkeys[at : at + 64, :].astype(jnp.bfloat16)
        for j in LEAVE[half * 4 : half * 4 + 4]:
            for s in (2, 1, 3):
                x_send(s, j).start()

    core_sends = []
    hops_y = (2, 1, 3, 0)

    def query_part(at):
        cols = pl.ds(pl.multiple_of(ymod(hops_y[at]) * 256, 256), 256)
        part = lax.dot_general(gscores[:, cols], keys[...], tn, preferred_element_type=jnp.float32) * SCALE
        dq_part[at] = part.reshape(2, 128, WIDTH)
        copy = remote(dq_part.at[at, 1 - k], dq_core.at[at], s_core.at[at], r_core.at[at], core)
        copy.start()
        core_sends.append(copy)

    def z_send(j):
        return remote(kslot(z_out, j), z_in.at[z], s_z.at[j], r_z.at[z], dev(z_=zmod(HOPS[j] - parity)))

    def sum_x(j):
        at = key_slot(0, j) * 16
        mine = dkeys[at : at + 16, :]
        for s in (1, 3, 2):
            x_send(s, j).wait_recv()
            mine = mine + x_in[s - 1, j * 16 : j * 16 + 16, :].astype(jnp.float32)
        dkeys[at : at + 16, :] = mine
        z_out[j * 16 : j * 16 + 16, :] = mine.astype(jnp.bfloat16)
        if j == OWN:
            pl.when(parity == 1)(lambda: z_send(OWN).start())
        else:
            z_send(j).start()

    for at in range(4):
        query_part(at)
    for j in LEAVE[:4]:
        sum_x(j)
    dq_sends = []
    for at, s in enumerate(hops_y[:3]):
        core_sends[at].wait_recv()
        dq_out[at] = (dq_part[at, k] + dq_core[at]).astype(jnp.bfloat16)
        copy = remote(dq_out.at[at], dq_in.at[at], s_dq.at[at], r_dq.at[at], dev(y_=ymod(s)))
        copy.start()
        dq_sends.append(copy)
    for j in LEAVE[4:]:
        sum_x(j)

    fin = [dev(xh_=1 - xh, y_=ymod(s)) for s in (2, 1, 3, 0)] + [dev(y_=ymod(s)) for s in (2, 1, 3)]

    def fin_send(slot, i, to):
        return remote(kslot(dc_ref, slot), kslot(dc_ref, slot), s_fin.at[i], r_fin.at[slot], to)

    def wait_fin(slot):
        fin_send(slot, 0, core).wait_recv()

    @pl.when(parity == 0)
    def _():
        at = key_slot(0, OWN) * 16
        acc = dkeys[at : at + 16, :]
        for s in NEAR:
            zz = zmod(s)
            remote(kslot(z_out, 0), z_in.at[zz], s_z.at[0], r_z.at[zz], core).wait_recv()
            acc = acc + z_in[zz].astype(jnp.float32)
        dc_ref[pl.ds(pl.multiple_of(g * 16, 16), 16), :] = acc.astype(jnp.bfloat16)
        for i, to in enumerate(fin):
            fin_send(g, i, to).start()

    core_sends[3].wait_recv()
    dq = dq_part[3, k] + dq_core[3]
    for copy in dq_sends:
        copy.wait_recv()
    for at in range(3):
        dq = dq + dq_in[at].astype(jnp.float32)
    dq_ref[...] = dq.astype(jnp.bfloat16)

    for i, s in enumerate((0, 1, 3, 2)):
        slot = ymod(s) * 2 + k
        if s == 0:
            pl.when(parity == 1)(lambda: wait_fin(slot))
        else:
            wait_fin(slot)
        fin_send(slot, 7 + i, core).start()
    for s in (0, 1, 3, 2):
        wait_fin(ymod(s) * 2 + 1 - k)

    @pl.when(parity == 0)
    def _():
        for s in FAR:
            send_key(s).wait_send()
        for i, to in enumerate(fin):
            fin_send(g, i, to).wait_send()

    for i in range(4):
        fin_send(g, 7 + i, core).wait_send()
    for copy in row_sends + stat_sends + core_sends + dq_sends:
        copy.wait_send()
    for j in range(8):
        for s in (2, 1, 3):
            forward(j, s).wait_send()
            x_send(s, j).wait_send()
        if j == OWN:
            pl.when(parity == 1)(lambda: z_send(OWN).wait_send())
        else:
            z_send(j).wait_send()


def on_device(queries, grad_out, latent_cache, slab_starts):
    f32, bf16 = jnp.float32, jnp.bfloat16
    dma = pltpu.SemaphoreType.DMA
    vmem = pl.BlockSpec(memory_space=pltpu.VMEM)
    query_grad, cache_grad = pl.pallas_call(
        kernel,
        out_shape=(
            jax.ShapeDtypeStruct((128, WIDTH), bf16),
            jax.ShapeDtypeStruct((128, WIDTH), bf16),
        ),
        in_specs=[pl.BlockSpec(memory_space=pltpu.SMEM), vmem, vmem, vmem],
        out_specs=[vmem, vmem],
        scratch_shapes=[
            pltpu.VMEM((1024, WIDTH), bf16),
            pltpu.VMEM((1024, LATENT), bf16),
            pltpu.VMEM((512, WIDTH), bf16),
            pltpu.VMEM((4, 512, 256), f32),
            pltpu.VMEM((4, 512, 256), f32),
            pltpu.VMEM((512, 1024), bf16),
            pltpu.VMEM((512, 1024), bf16),
            pltpu.VMEM((512, WIDTH), f32),
            pltpu.VMEM((8, 2, 16, 128), f32),
            pltpu.VMEM((4, 2, 128, WIDTH), f32),
            pltpu.VMEM((4, 128, WIDTH), f32),
            pltpu.VMEM((3, 128, WIDTH), bf16),
            pltpu.VMEM((3, 128, WIDTH), bf16),
            pltpu.VMEM((3, 128, WIDTH), bf16),
            pltpu.VMEM((3, 128, WIDTH), bf16),
            pltpu.VMEM((128, WIDTH), bf16),
            pltpu.VMEM((16, 16, WIDTH), bf16),
            dma((14,)), dma((8,)), dma((8,)),
            dma((16,)), dma((8,)), dma((8, 3)), dma((4, 8)),
            dma((2, 8)), dma((2, 8)),
            dma((4,)), dma((4,)), dma((3,)), dma((3,)),
            dma((3, 8)), dma((3, 8)), dma((8,)), dma((16,)),
            dma((11,)), dma((8,)),
        ],
        compiler_params=pltpu.CompilerParams(
            collective_id=0, has_side_effects=True, vmem_limit_bytes=40 << 20
        ),
        cost_estimate=pl.CostEstimate(flops=2886000000, bytes_accessed=900000, transcendentals=530000),
        name="latent_attention_backward",
    )(
        slab_starts,
        queries.reshape(128, WIDTH),
        grad_out.reshape(128, LATENT),
        latent_cache,
    )
    return query_grad.reshape(queries.shape), cache_grad.astype(f32)


def solution(mesh):
    placed = (P("ctx", "tp", None), P("ctx", "tp", None), P("ctx", None), P("ctx"))
    return jax.shard_map(
        on_device,
        mesh=mesh,
        in_specs=placed,
        out_specs=(P("ctx", "tp", None), P("ctx", None)),
        check_vma=False,
    )
```
